256 devices in a mesh: tile: 32 (over z, x), scan: 8 (over y, core).
Axes of the slice: x: 4, y: 4, z: 8, core: 2. Of those that a mesh axis runs over, the one named last changes fastest.
Arguments:
- object_field: float32 [2, 2, 512, 16384], P(None, None, None, 'tile'), may hold values from -1 to 1
- probe_wavefield: float32 [2, 2, 256, 256], replicated, may hold values from -3 to 3
- measured: float32 [32, 8, 2, 256, 256], P('tile', 'scan'), may hold values from 0 to 1
- offsets: int32 [32, 8, 2, 2], P('tile', 'scan'), may hold values from 0 to 511, as said below
- counts: int32 [32, 8], P('tile', 'scan'), may hold values from 0 to 2, as said below
Outputs:
- object_gradient: float32 [2, 2, 512, 16384], P(None, None, 'scan', 'tile')
- probe_gradient: float32 [2, 2, 256, 256], replicated
The draws below stay inside these ranges and needn't reach their ends.
Inputs may be any that keep to these rules, and one draw needn't show every extreme that they name: `offsets`: offsets keep a window within the strip of its tile index and the next strip: row up to 256, column up to 511, and column up to 256 on the last tile index. The counts of the devices with one tile index sum to the number of scan groups.
All inputs are finite; a program needn't handle non-finite values.
Results may differ from the reference program's by a relative error of at most 0.0003.
Values sent between devices are 32-bit elements; how exact they have to be, the bound alone decides.
No kernel may reach another device: no remote copies, remote signals or barrier semaphores. Data moves between devices by JAX's collectives and lax.ppermute only.
A program may use at most 128 MiB of HBM per device.

```python
import math
import jax
import jax.numpy as jnp
from jax import lax

PROBE_WIDTH = 256
M = 2
L = 2
CAP = 2
NY = 512
SW = 512
NX = 16384
N_TILE = 32
N_SCAN = 8


def draw_offsets(key, part):
    key = jax.random.fold_in(key, 11)
    key_rows, key_cols = jax.random.split(key)
    row_draw = jax.random.randint(key_rows, (N_TILE, N_SCAN, CAP), 0, NY - PROBE_WIDTH + 1)
    col_draw = jax.random.randint(key_cols, (N_TILE, N_SCAN, CAP), 0, SW)
    last_tile = jnp.arange(N_TILE)[:, None, None] == N_TILE - 1
    col_draw = jnp.where(last_tile, col_draw % (SW - PROBE_WIDTH + 1), col_draw)
    row_draw = row_draw.at[0, 0, 0].set(NY - PROBE_WIDTH).at[1, 0, 0].set(0)
    col_draw = col_draw.at[0, 0, 0].set(SW - 1).at[1, 0, 0].set(0)
    return jnp.stack([row_draw, col_draw], axis=-1).astype(jnp.int32)


def draw_counts(key, part):
    key = jax.random.fold_in(key, 23)
    key_many, key_order = jax.random.split(key)
    doubles = jax.random.randint(key_many, (N_TILE, 1), 1, N_SCAN // 2 + 1)
    scores = jax.random.randint(key_order, (N_TILE, N_SCAN), 0, 1 << 20) * N_SCAN + jnp.arange(N_SCAN)[None, :]
    ranking = jnp.argsort(jnp.argsort(scores, axis=1), axis=1)
    filled = jnp.where(ranking < doubles, CAP, jnp.where(ranking < 2 * doubles, 0, 1))
    return filled.astype(jnp.int32)


def level_of(rng, shape, shards, least, largest):
    def one(position, shards_of):
        draws = jax.random.uniform(jax.random.fold_in(jax.random.fold_in(rng, 6), position), (shards_of,), jnp.float32, least / len(shards), largest / len(shards))
        return jnp.repeat(jnp.exp(draws), shape[position] // shards_of).reshape((-1,) + (1,) * (len(shape) - position - 1))

    level = one(*shards[0])
    for cut in shards[1:]:
        level = level * one(*cut)
    return level


def normal_values(key, extent, width, bound, kind=jnp.bfloat16):
    array = jax.random.normal(key, extent, jnp.float32) * width
    return jnp.minimum(jnp.maximum(array, -bound), bound).astype(kind)


def setup_inputs(seed: int = 0) -> dict:
    keys = jax.random.split(jax.random.key(seed), 6)
    return {
        "object_field": jnp.clip(jax.random.uniform(keys[0], (2, L, NY, NX), jnp.float32, -1.0, 1.0) * level_of(keys[0], (2, L, NY, NX), ((3, 32),), -0.4, 0.0), -1.0, 1.0),
        "probe_wavefield": normal_values(keys[1], (2, M, PROBE_WIDTH, PROBE_WIDTH), 0.5, 3.0, jnp.float32),
        "measured": jnp.clip(1.0 * jax.random.uniform(keys[2], (N_TILE, N_SCAN, CAP, PROBE_WIDTH, PROBE_WIDTH), jnp.float32) ** level_of(keys[2], (N_TILE, N_SCAN, CAP, PROBE_WIDTH, PROBE_WIDTH), ((0, 32), (1, 8)), -0.2, 0.2), 0.0, 1.0),
        "offsets": draw_offsets(jax.random.fold_in(keys[5], 71), 0),
        "counts": draw_counts(jax.random.fold_in(keys[5], 71), 0),
    }


def precise_matmul(left_pair, right_pair):
    return jnp.matmul(left_pair, right_pair, precision=lax.Precision.HIGHEST)

def mat_product(left_pair, right_pair):
    real_part = precise_matmul(left_pair[0], right_pair[0]) - precise_matmul(left_pair[1], right_pair[1])
    imag_part = precise_matmul(left_pair[0], right_pair[1]) + precise_matmul(left_pair[1], right_pair[0])
    return (real_part, imag_part)

def transform(field_pair, table):
    return mat_product(table, mat_product(field_pair, table))

def complex_times(left_pair, right_pair):
    return (left_pair[0] * right_pair[0] - left_pair[1] * right_pair[1], left_pair[0] * right_pair[1] + left_pair[1] * right_pair[0])

def times_conj(left_pair, right_pair):
    return (left_pair[0] * right_pair[0] + left_pair[1] * right_pair[1], left_pair[1] * right_pair[0] - left_pair[0] * right_pair[1])

def make_tables(length):
    indices = jnp.arange(length, dtype=jnp.int32)
    phase_steps = indices[:, None] * indices[None, :] % length
    angles = 2.0 * math.pi / length * phase_steps.astype(jnp.float32)
    norm_scale = 1.0 / math.sqrt(length)
    forward_table = (jnp.cos(angles) * norm_scale, -jnp.sin(angles) * norm_scale)
    inverse_table = (forward_table[0], -forward_table[1])
    frequency = (indices + length // 2) % length - length // 2
    square = (frequency[:, None] * frequency[:, None] + frequency[None, :] * frequency[None, :]) % (4 * length)
    chirp_phase = 2.0 * math.pi / (4 * length) * square.astype(jnp.float32)
    transfer = (jnp.cos(chirp_phase), -jnp.sin(chirp_phase))
    return (forward_table, inverse_table, transfer)

def propagate(field_pair, lookup_tables):
    return transform(complex_times(transform(field_pair, lookup_tables[0]), lookup_tables[2]), lookup_tables[1])

def back_propagate(field_pair, lookup_tables):
    return transform(times_conj(transform(field_pair, lookup_tables[0]), lookup_tables[2]), lookup_tables[1])

def position_terms(window, probe_wavefield, measured_map, active_marker, lookup_tables):
    layers = window.shape[1]
    incoming = []
    field_now = (probe_wavefield[0], probe_wavefield[1])
    for depth_index in range(layers):
        if depth_index > 0:
            field_now = propagate(field_now, lookup_tables)
        incoming.append(field_now)
        field_now = complex_times(field_now, (window[0, depth_index], window[1, depth_index]))
    far_field = transform(field_now, lookup_tables[0])
    intensity = lax.optimization_barrier(jnp.sum(far_field[0] * far_field[0] + far_field[1] * far_field[1], axis=0))
    misfit = (intensity - measured_map) * active_marker
    back_wave = transform((far_field[0] * misfit, far_field[1] * misfit), lookup_tables[1])
    layer_grads = []
    for depth_index in reversed(range(layers)):
        product_term = times_conj(back_wave, incoming[depth_index])
        layer_grads.append(jnp.stack([lax.optimization_barrier(jnp.sum(product_term[0], axis=0)), lax.optimization_barrier(jnp.sum(product_term[1], axis=0))]))
        back_wave = times_conj(back_wave, (window[0, depth_index], window[1, depth_index]))
        if depth_index > 0:
            back_wave = back_propagate(back_wave, lookup_tables)
    patch_grad = jnp.stack(layer_grads[::-1], axis=1)
    return (patch_grad, jnp.stack([back_wave[0], back_wave[1]]))

def reference(object_field, probe_wavefield, measured, offsets, counts):
    lookup_tables = make_tables(PROBE_WIDTH)
    position_count = N_TILE * N_SCAN * CAP
    flattened_measurements = measured.reshape(position_count, PROBE_WIDTH, PROBE_WIDTH)
    flattened_scan_offsets = offsets.reshape(position_count, 2)
    patch_index_list = jnp.repeat(jnp.arange(N_TILE, dtype=jnp.int32), N_SCAN * CAP)
    slot_ids = jnp.tile(jnp.arange(CAP, dtype=jnp.int32), N_TILE * N_SCAN)
    active_index_list = (slot_ids < jnp.repeat(counts.reshape(N_TILE * N_SCAN), CAP)).astype(jnp.int32)
    zero_index = jnp.zeros((), jnp.int32)

    def compute(operands):
        return position_terms(operands[0], probe_wavefield, operands[1], jnp.float32(1.0), lookup_tables)

    def skipped(operands):
        return (jnp.zeros((2, L, PROBE_WIDTH, PROBE_WIDTH), jnp.float32), jnp.zeros((2, M, PROBE_WIDTH, PROBE_WIDTH), jnp.float32))

    def process_position(running, element):
        grad_obj, grad_probe = running
        measured_map, offset_pair, tile_id, alive_id = element
        corner = (zero_index, zero_index, offset_pair[0].astype(jnp.int32), (tile_id * SW + offset_pair[1]).astype(jnp.int32))
        window = lax.dynamic_slice(object_field, corner, (2, L, PROBE_WIDTH, PROBE_WIDTH))
        patch_grad, probe_part = lax.cond(alive_id > 0, compute, skipped, (window, measured_map))
        current = lax.dynamic_slice(grad_obj, corner, (2, L, PROBE_WIDTH, PROBE_WIDTH))
        grad_obj = lax.dynamic_update_slice(grad_obj, current + patch_grad, corner)
        return ((grad_obj, grad_probe + probe_part), None)
    initial_state = (jnp.zeros((2, L, NY, NX), jnp.float32), jnp.zeros((2, M, PROBE_WIDTH, PROBE_WIDTH), jnp.float32))
    ending_state, discarded_value = lax.scan(process_position, initial_state, (flattened_measurements, flattened_scan_offsets, patch_index_list, active_index_list))
    return (ending_state[0], ending_state[1] / math.sqrt(N_TILE * N_SCAN))
```

```python
import math

import jax
import jax.numpy as jnp
import ml_dtypes
import numpy as np
from jax import lax
from jax.experimental import pallas as pl
from jax.experimental.pallas import tpu as pltpu
from jax.sharding import PartitionSpec as P

BF = jnp.bfloat16
F32 = jnp.float32
VMEM_BYTES = 40 << 20


def split_table(table):
    high = table.astype(ml_dtypes.bfloat16)
    low = (table - high.astype(np.float64)).astype(ml_dtypes.bfloat16)
    return high, low


def make_tables(n):
    j = np.arange(n)
    phase = 2 * np.pi * ((j[:, None] * j[None, :]) % n) / n
    cas = (np.cos(phase) + np.sin(phase)) / math.sqrt(n)
    sigma = np.concatenate([np.arange(n // 2), [n // 2], np.arange(n - 1, n // 2, -1)])
    high, low = split_table(cas)
    phigh, plow = split_table(cas[sigma])
    left = np.concatenate([high, high, low], 1)
    right = np.concatenate([high, high, low], 0)
    left_in = np.concatenate([phigh, phigh, plow], 1)
    right_in = np.concatenate([phigh.T, phigh.T, plow.T], 0)
    left_out = np.concatenate([phigh.T, phigh.T, plow.T], 1)
    right_out = np.concatenate([phigh, phigh, plow], 0)
    f = (j + n // 2) % n - n // 2
    q = (f[:, None] ** 2 + f[None, :] ** 2) % (4 * n)
    chirp = 2 * np.pi * q / (4 * n)
    transfer = np.stack([np.cos(chirp), -np.sin(chirp)]).astype(np.float32)
    perm = np.zeros((n, n))
    perm[j, sigma] = 1
    return {
        "plain": (left, right),
        "far": (left_in, right_in),
        "back": (left_out, right_out),
        "transfer": transfer,
        "perm": perm.astype(ml_dtypes.bfloat16),
    }


def split(x):
    high = x.astype(BF)
    return high, (x - high.astype(F32)).astype(BF)


def dot(a, b):
    return jnp.dot(a, b, preferred_element_type=F32)


def right_mul(x, table):
    high, low = split(x)
    return dot(jnp.concatenate([high, low, high], 1), table)


def left_mul(table, x):
    high, low = split(x)
    return dot(table, jnp.concatenate([high, low, high], 0))


def two_sided(pair, tables):
    return tuple(left_mul(tables[0][...], right_mul(p, tables[1][...])) for p in pair)


def cmul(a, b):
    return a[0] * b[0] - a[1] * b[1], a[0] * b[1] + a[1] * b[0]


def cmulc(a, b):
    return a[0] * b[0] + a[1] * b[1], a[1] * b[0] - a[0] * b[1]


def swap_rows(z):
    n = z.shape[0]
    h = n // 2
    fixed = lax.broadcasted_iota(jnp.int32, z.shape, 0) % h == 0
    return jnp.where(fixed, z, jnp.concatenate([z[h:], z[:h]], 0))


def swap_cols(z):
    n = z.shape[1]
    h = n // 2
    fixed = lax.broadcasted_iota(jnp.int32, z.shape, 1) % h == 0
    return jnp.where(fixed, z, jnp.concatenate([z[:, h:], z[:, :h]], 1))


def mix(pair, sign):
    a, b = pair
    ca, cb = swap_cols(a), swap_cols(b)
    re = 0.5 * (sign * (b - swap_rows(cb)) + (swap_rows(a) + ca))
    im = 0.5 * (sign * (swap_rows(ca) - a) + (swap_rows(b) + cb))
    return re, im


def corner_of(offs, slot, rows):
    r, c = offs[2 * slot], offs[2 * slot + 1]
    row = jnp.minimum(lax.div(r, 8), rows // 8 - 33) * 8
    col = lax.div(c, 128) * 128
    return pl.multiple_of(row, 8), pl.multiple_of(col, 128), r - row, c - col


def take_window(ext, offs, slot, part):
    row, col, dr, dc = corner_of(offs, slot, ext.shape[1])
    x = ext[part, pl.ds(row, 264), pl.ds(col, 384)]
    x = pltpu.roll(x, lax.rem(384 - dc, 384), 1)
    x = pltpu.roll(x, lax.rem(264 - dr, 264), 0)
    return x[:256, :256]


def add_window(acc, offs, slot, part, g):
    row, col, dr, dc = corner_of(offs, slot, acc.shape[1])
    x = jnp.pad(g, ((0, 8), (0, 128)))
    x = pltpu.roll(x, dc, 1)
    x = pltpu.roll(x, dr, 0)
    acc[part, pl.ds(row, 264), pl.ds(col, 384)] += x


def load_ext(strip, layer, pieces, offs, ext, sem):
    copy = pltpu.make_async_copy(strip.at[:, layer], ext.at[:, :, pl.ds(0, 512)], sem)
    copy.start()
    y, c = offs[4], offs[5]
    half = lax.rem(y, 2)
    for k, piece in enumerate(pieces):
        hh = half if k % 2 == 0 else 1 - half
        cc = c if k < 2 else 1 - c
        row = pl.multiple_of(256 * hh + 128 * cc, 128)
        ext[:, pl.ds(row, 128), pl.ds(512, 256)] = piece[...]
    copy.wait()


def propagate_kernel(offs, strip, h0, h1, h2, h3, probe, tl, tr, transfer, o1, u, ext, sem):
    load_ext(strip, 0, (h0, h1, h2, h3), offs, ext, sem)

    @pl.loop(0, 2)
    def _(slot):
        @pl.when(slot < offs[6])
        def _():
            for part in range(2):
                o1[slot, part] = take_window(ext, offs, slot, part)
            obj = (o1[slot, 0], o1[slot, 1])
            h = (transfer[0], transfer[1])
            for m in range(2):
                w = cmul((probe[0, m], probe[1, m]), obj)
                z = cmul(two_sided(w, (tl, tr)), h)
                g = two_sided(z, (tl, tr))
                u[slot, m, 0] = g[0]
                u[slot, m, 1] = g[1]


def write_blocks(acc, offs, keep, send, keep_sib, send_sib):
    y, c = offs[4], offs[5]
    a, b = jnp.bitwise_xor(y, 1), 3 - y
    p = jnp.where(c == 0, a, b)
    o = jnp.where(c == 0, b, a)
    q = 3 - a

    def block(chip, core):
        row = pl.multiple_of(128 * chip + 64 * core, 64)
        return acc[:, pl.ds(row, 64), :]

    send_sib[0] = block(o, 1 - c)
    send_sib[1] = block(q, 1 - c)
    send[0] = block(p, c)
    send[1] = block(q, c)
    keep_sib[0] = block(y, 1 - c)
    keep_sib[1] = block(p, 1 - c)
    keep[0] = block(y, c)
    keep[1] = block(o, c)


def far_kernel(
    offs, strip, h0, h1, h2, h3, u, meas, perm, fl, fr, bl, br,
    c2, keep, send, keep_sib, send_sib, ext, acc, psi, sem,
):
    load_ext(strip, 1, (h0, h1, h2, h3), offs, ext, sem)
    acc[...] = jnp.zeros_like(acc)

    @pl.loop(0, 2)
    def _(slot):
        @pl.when(slot < offs[6])
        def _():
            obj = tuple(take_window(ext, offs, slot, part) for part in range(2))
            pm = perm[...]
            high, low = split(meas[slot])
            high, low = split(dot(pm, high) + dot(pm, low))
            dims = (((1,), (1,)), ((), ()))
            misfit = -(
                lax.dot_general(high, pm, dims, preferred_element_type=F32)
                + lax.dot_general(low, pm, dims, preferred_element_type=F32)
            )
            for m in range(2):
                w = cmul((u[slot, m, 0], u[slot, m, 1]), obj)
                re, im = mix(two_sided(w, (fl, fr)), 1.0)
                psi[m, 0] = re
                psi[m, 1] = im
                misfit = misfit + (re * re + im * im)
            total = None
            for m in range(2):
                v = mix((psi[m, 0] * misfit, psi[m, 1] * misfit), -1.0)
                g = two_sided(v, (bl, br))
                term = cmulc(g, (u[slot, m, 0], u[slot, m, 1]))
                total = term if total is None else (total[0] + term[0], total[1] + term[1])
                c = cmulc(g, obj)
                c2[slot, m, 0] = c[0]
                c2[slot, m, 1] = c[1]
            for part in range(2):
                add_window(acc, offs, slot, part, total[part])

    write_blocks(acc, offs, keep, send, keep_sib, send_sib)


def back_kernel(
    offs, c2, o1, probe, tl, tr, transfer,
    mine, sib, keep, send, keep_sib, send_sib, acc, pacc,
):
    acc[...] = jnp.zeros_like(acc)
    pacc[...] = jnp.zeros_like(pacc)

    @pl.loop(0, 2)
    def _(slot):
        @pl.when(slot < offs[6])
        def _():
            obj = (o1[slot, 0], o1[slot, 1])
            h = (transfer[0], transfer[1])
            total = None
            for m in range(2):
                z = cmulc(two_sided((c2[slot, m, 0], c2[slot, m, 1]), (tl, tr)), h)
                g = two_sided(z, (tl, tr))
                term = cmulc(g, (probe[0, m], probe[1, m]))
                total = term if total is None else (total[0] + term[0], total[1] + term[1])
                c = cmulc(g, obj)
                pacc[m, 0] += c[0]
                pacc[m, 1] += c[1]
            for part in range(2):
                add_window(acc, offs, slot, part, total[part])

    c = offs[5]
    mine[...] = pacc[c]
    sib[...] = pacc[1 - c]
    write_blocks(acc, offs, keep, send, keep_sib, send_sib)


def struct(*shape):
    return jax.ShapeDtypeStruct(shape, F32)


def run_kernel(body, name, ins, outs, scratch, flops, n_any=()):
    specs = []
    for i in range(len(ins)):
        if i == 0:
            specs.append(pl.BlockSpec(memory_space=pltpu.SMEM))
        elif i in n_any:
            specs.append(pl.BlockSpec(memory_space=pl.ANY))
        else:
            specs.append(pl.BlockSpec(memory_space=pltpu.VMEM))
    return pl.pallas_call(
        body,
        out_shape=outs,
        in_specs=specs,
        out_specs=[pl.BlockSpec(memory_space=pltpu.VMEM)] * len(outs),
        scratch_shapes=scratch,
        compiler_params=pltpu.CompilerParams(vmem_limit_bytes=VMEM_BYTES),
        cost_estimate=pl.CostEstimate(flops=flops, bytes_accessed=8 << 20, transcendentals=0),
        name=name,
    )(*ins)


def pairs(n, f):
    return [(i, f(i)) for i in range(n)]


def core_swap(x):
    return lax.ppermute(x, "c", [(0, 1), (1, 0)])


def pattern(first):
    def f(i):
        y, c = i // 2, i % 2
        return 2 * ((y ^ 1) if (c == 0) == first else 3 - y) + c

    return pairs(8, f)


def y_swap(x, first):
    return lax.ppermute(x, ("y", "c"), pattern(first))


def tile_shift(x, by):
    n = lax.axis_size("z") * lax.axis_size("x")
    return lax.ppermute(x, ("z", "x"), [(i, i + by) for i in range(n) if 0 <= i + by < n])


def reduce_rows(keep, send, keep_sib, send_sib):
    got_send = core_swap(send_sib)
    got_keep = core_swap(keep_sib)
    got = y_swap(send + got_send, True)
    kept = keep + got_keep + got
    return kept[0] + y_swap(kept[1], False)


def finish(rows):
    edge = tile_shift(rows[:, :, 512:], 1)
    return jnp.concatenate([rows[:, :, :256] + edge, rows[:, :, 256:512]], 2)


def shards(object_field, probe, measured, offsets, counts):
    n = probe.shape[-1]
    tables = make_tables(n)
    y, c = lax.axis_index("y"), lax.axis_index("c")
    offs = jnp.concatenate(
        [offsets.reshape(4), y.astype(jnp.int32)[None], c.astype(jnp.int32)[None], counts.reshape(1)]
    )
    zero = jnp.zeros((), jnp.int32)
    row = (256 * lax.rem(y, 2) + 128 * c).astype(jnp.int32)
    halos = []
    for layer in range(2):
        part = lax.dynamic_slice(object_field[:, layer], (zero, row, zero), (2, 128, n))
        halos.append(tile_shift(part, -1))
    pieces = []
    for got in halos:
        other = y_swap(got, True)
        pieces.append((got, other, core_swap(got), core_swap(other)))

    tl, tr = (jnp.asarray(t) for t in tables["plain"])
    fl, fr = (jnp.asarray(t) for t in tables["far"])
    bl, br = (jnp.asarray(t) for t in tables["back"])
    transfer = jnp.asarray(tables["transfer"])
    perm = jnp.asarray(tables["perm"])
    meas = measured[0, 0]
    ext = pltpu.VMEM((2, 512, 768), F32)
    sem = pltpu.SemaphoreType.DMA(())
    blocks = [struct(2, 2, 64, 768)] * 4
    flops = 16 * 3 * 2 * n**3
    o1, u = run_kernel(
        propagate_kernel, "propagate",
        (offs, object_field, *pieces[0], probe, tl, tr, transfer),
        [struct(2, 2, n, n), struct(2, 2, 2, n, n)],
        [ext, sem], 2 * flops, n_any=(1,),
    )
    c2, *far_blocks = run_kernel(
        far_kernel, "far_field",
        (offs, object_field, *pieces[1], u, meas, perm, fl, fr, bl, br),
        [struct(2, 2, 2, n, n)] + blocks,
        [ext, pltpu.VMEM((2, 512, 768), F32), pltpu.VMEM((2, 2, n, n), F32), sem],
        2 * flops, n_any=(1,),
    )
    mine, sib, *near_blocks = run_kernel(
        back_kernel, "back",
        (offs, c2, o1, probe, tl, tr, transfer),
        [struct(2, n, n), struct(2, n, n)] + blocks,
        [pltpu.VMEM((2, 512, 768), F32), pltpu.VMEM((2, 2, n, n), F32)],
        2 * flops,
    )

    total = (mine + core_swap(sib)).reshape(16, 64, 128)
    total = jnp.sum(lax.all_to_all(total, ("x", "y"), 0, 0, tiled=True), axis=0)
    total = jnp.broadcast_to(total, (8, 64, 128))
    total = jnp.sum(lax.all_to_all(total, "z", 0, 0, tiled=True), axis=0) * (1.0 / 16.0)
    total = jnp.broadcast_to(total, (16, 64, 128))
    total = lax.all_to_all(total, ("x", "y"), 0, 0, tiled=True).reshape(2, n, n)
    other = core_swap(total)
    first = jnp.where(c == 0, total, other)
    second = jnp.where(c == 0, other, total)
    probe_gradient = jnp.stack([first, second], axis=1)

    far_rows = finish(reduce_rows(*far_blocks))
    near_rows = finish(reduce_rows(*near_blocks))
    return jnp.stack([near_rows, far_rows], axis=1), probe_gradient


def solution(mesh):
    sizes = (8, 4, 4, 2)
    split_mesh = jax.sharding.Mesh(mesh.devices.reshape(sizes), ("z", "x", "y", "c"))
    tile, scan = ("z", "x"), ("y", "c")
    in_specs = (
        P(None, None, None, tile),
        P(),
        P(tile, scan, None, None, None),
        P(tile, scan, None, None),
        P(tile, scan),
    )
    out_specs = (P(None, None, scan, tile), P())
    return jax.shard_map(
        shards, mesh=split_mesh, in_specs=in_specs, out_specs=out_specs, check_vma=False
    )
```

```python
import math

import jax
import jax.numpy as jnp
import ml_dtypes
import numpy as np
from jax import lax
from jax.experimental import pallas as pl
from jax.experimental.pallas import tpu as pltpu
from jax.sharding import PartitionSpec as P

BF = jnp.bfloat16
F32 = jnp.float32
LONG = 1 << 35


def split_table(table):
    high = table.astype(ml_dtypes.bfloat16)
    low = (table - high.astype(np.float64)).astype(ml_dtypes.bfloat16)
    return high, low


def make_tables(n):
    h = n // 2
    even = np.concatenate([np.arange(0, h, 2), [h], np.arange(n - 2, h, -2)])
    odd = np.concatenate([np.arange(1, h, 2), np.arange(n - 1, h, -2)])
    order = np.concatenate([even, odd])
    pixel = np.arange(n)
    blocks = []
    for rows in (even, odd):
        phase = 2 * np.pi * ((rows[:, None] * pixel[None, :h]) % n) / n
        blocks.append((np.cos(phase) + np.sin(phase)) / math.sqrt(n))

    def square(block):
        high, low = split_table(block)
        half = np.concatenate([high, low], 1)
        return np.concatenate([half, half], 0)

    squares = []
    for block in blocks:
        squares += [square(block.T).T, square(block.T), square(block).T, square(block)]
    perm = np.zeros((n, n))
    perm[pixel, order] = 1
    squares.append(perm.astype(ml_dtypes.bfloat16))
    f = (order + h) % n - h
    q = (f[:, None] ** 2 + f[None, :] ** 2) % (4 * n)
    chirp = 2 * np.pi * q / (4 * n)
    transfer = np.stack([np.cos(chirp), -np.sin(chirp)]).astype(np.float32)
    return np.stack(squares), transfer


def split(x):
    high = x.astype(BF)
    return high, (x - high.astype(F32)).astype(BF)


def dot(a, b):
    return jnp.dot(a, b, preferred_element_type=F32)


def columns_by(x, table):
    high, low = split(x)
    y = dot(jnp.concatenate([high, low], 1), table)
    h = x.shape[1]
    return y[:, :h] + y[:, h:]


def rows_by(table, x):
    high, low = split(x)
    y = dot(table, jnp.concatenate([high, low], 0))
    h = x.shape[0]
    return y[:h] + y[h:]


def to_frequency(planes, tables):
    h = planes[0].shape[0] // 2
    even = [columns_by(x[:, :h] + x[:, h:], tables[1]) for x in planes]
    odd = [columns_by(x[:, :h] - x[:, h:], tables[5]) for x in planes]
    planes = [jnp.concatenate(p, 1) for p in zip(even, odd)]
    even = [rows_by(tables[0], x[:h] + x[h:]) for x in planes]
    odd = [rows_by(tables[4], x[:h] - x[h:]) for x in planes]
    return [jnp.concatenate(p, 0) for p in zip(even, odd)]


def to_pixels(planes, tables):
    h = planes[0].shape[0] // 2
    a = [columns_by(x[:, :h], tables[3]) for x in planes]
    b = [columns_by(x[:, h:], tables[7]) for x in planes]
    planes = [jnp.concatenate([p + q, p - q], 1) for p, q in zip(a, b)]
    a = [rows_by(tables[2], x[:h]) for x in planes]
    b = [rows_by(tables[6], x[h:]) for x in planes]
    return [jnp.concatenate([p + q, p - q], 0) for p, q in zip(a, b)]


def cmul(a, b):
    return a[0] * b[0] - a[1] * b[1], a[0] * b[1] + a[1] * b[0]


def cmulc(a, b):
    return a[0] * b[0] + a[1] * b[1], a[1] * b[0] - a[0] * b[1]


def swap_rows(z):
    q = z.shape[0] // 4
    row = lax.broadcasted_iota(jnp.int32, z.shape, 0)
    fixed = jnp.logical_or(row == 0, row == q)
    turned = jnp.concatenate([z[q : 2 * q], z[:q], z[3 * q :], z[2 * q : 3 * q]], 0)
    return jnp.where(fixed, z, turned)


def swap_cols(z):
    q = z.shape[1] // 4
    even, odd = z[:, : 2 * q], z[:, 2 * q :]
    col = lax.broadcasted_iota(jnp.int32, even.shape, 1)
    fixed = jnp.logical_or(col == 0, col == q)
    even = jnp.where(fixed, even, pltpu.roll(even, q, 1))
    return jnp.concatenate([even, pltpu.roll(odd, q, 1)], 1)


def mix(pair, sign):
    a, b = pair
    ca, cb = swap_cols(a), swap_cols(b)
    re = 0.5 * (sign * (b - swap_rows(cb)) + (swap_rows(a) + ca))
    im = 0.5 * (sign * (swap_rows(ca) - a) + (swap_rows(b) + cb))
    return re, im


def corner_of(r, c, rows):
    row = jnp.minimum(lax.div(r, 8), rows // 8 - 33) * 8
    col = lax.div(c, 128) * 128
    return pl.multiple_of(row, 8), pl.multiple_of(col, 128), r - row, c - col


def partners(y, c):
    near, far = jnp.bitwise_xor(y, 1), 3 - y
    return jnp.where(c == 0, near, far), jnp.where(c == 0, far, near), 3 - near


def plan_kernel(info, me, plan, token):
    count = [info[s, 0, 0] for s in range(8)]
    zeros, doubles = jnp.int32(0), jnp.int32(0)
    zero_rank, double_rank = [], []
    for s in range(8):
        zero_rank.append(zeros)
        double_rank.append(doubles)
        zeros = zeros + (count[s] == 0).astype(jnp.int32)
        doubles = doubles + (count[s] == 2).astype(jnp.int32)
    for s in range(8):
        source = jnp.int32(0)
        for e in range(8):
            taken = jnp.logical_and(count[e] == 2, double_rank[e] == zero_rank[s])
            source = jnp.where(taken, e, source)
        away = count[s] == 0
        source = jnp.where(away, source, s)
        slot = away.astype(jnp.int32)
        plan[s, 0] = source
        plan[s, 1] = slot
        plan[s, 2] = info[source, 0, 1 + 2 * slot]
        plan[s, 3] = info[source, 0, 2 + 2 * slot]
    token[...] = jnp.zeros_like(token)
    plan[8, 0] = me[0, 5]
    plan[8, 1] = me[0, 6]


def pick_kernel(plan, mine_1, got_a, got_b, for_sib, sem):
    y, c = plan[8, 0], plan[8, 1]
    source = plan[2 * y + 1 - c, 0]
    a, b, e = partners(y, c)

    def give(device, ref):
        @pl.when(source == device)
        def _():
            copy = pltpu.make_async_copy(ref, for_sib, sem)
            copy.start()
            copy.wait()

    give(2 * y + c, mine_1)
    give(2 * a + c, got_a)
    give(2 * b + c, got_b.at[0])
    give(2 * e + c, got_b.at[1])


def tie_kernel(*refs):
    pass


def join_kernel(*refs):
    refs[-1][...] = jnp.zeros_like(refs[-1])


def compute_kernel(
    plan, joined, strip, h00, h01, h02, h03, h10, h11, h12, h13, probe,
    mine_0, mine_1, got_a, got_b, got_sib, tables, transfer,
    grad, mine, sib, halo, full, obj, us, psi, meas, sem,
):
    y, c = plan[8, 0], plan[8, 1]
    own = 2 * y + c
    source, slot = plan[own, 0], plan[own, 1]
    row, col, dr, dc = corner_of(plan[own, 2], plan[own, 3], 512)
    first = lax.div(col, 128)

    a, b, e = partners(y, c)
    core = lax.rem(source, 2)
    chip = lax.div(source, 2)
    here = jnp.logical_and(slot == 1, core == c)
    choices = [
        (slot == 0, mine_0),
        (jnp.logical_and(here, chip == y), mine_1),
        (jnp.logical_and(here, chip == a), got_a),
        (jnp.logical_and(here, chip == b), got_b.at[0]),
        (jnp.logical_and(here, chip == e), got_b.at[1]),
        (jnp.logical_and(slot == 1, core != c), got_sib),
    ]
    for chosen, ref in choices:

        @pl.when(chosen)
        def _():
            pltpu.make_async_copy(ref, meas, sem).start()

    half = lax.rem(y, 2)
    for layer, pieces in enumerate(((h00, h01, h02, h03), (h10, h11, h12, h13))):
        for k, piece in enumerate(pieces):
            hh = half if k % 2 == 0 else 1 - half
            cc = c if k < 2 else 1 - c
            at = pl.multiple_of(256 * hh + 128 * cc, 128)
            halo[:, layer, pl.ds(at, 128), :] = piece[...]
    for i in range(3):

        @pl.when(first + i >= 4)
        def _():
            cols = pl.multiple_of(128 * (first + i - 4), 128)
            full[:, :, :, 128 * i : 128 * (i + 1)] = halo[:, :, pl.ds(row, 264), pl.ds(cols, 128)]

        @pl.when(first + i < 4)
        def _():
            cols = pl.multiple_of(col + 128 * i, 128)
            full[:, :, :, 128 * i : 128 * (i + 1)] = strip[:, :, pl.ds(row, 264), pl.ds(cols, 128)]

    def window(layer):
        for part in range(2):
            x = pltpu.roll(full[part, layer], lax.rem(384 - dc, 384), 1)[:, :256]
            x = pltpu.roll(x, lax.rem(264 - dr, 264), 0)
            obj[layer, part] = x[:256]

    def load(ref, *index):
        return ref[(*index, 0)], ref[(*index, 1)]

    def modes(planes):
        return (planes[0], planes[1]), (planes[2], planes[3])

    def chirped(product, planes):
        h = (transfer[0], transfer[1])
        return [x for pair in modes(planes) for x in product(pair, h)]

    window(0)
    planes = [x for m in range(2) for x in cmul((probe[0, m], probe[1, m]), load(obj, 0))]
    planes = to_pixels(chirped(cmul, to_frequency(planes, tables)), tables)
    for k in range(4):
        us[k // 2, k % 2] = planes[k]
    window(1)
    pltpu.make_async_copy(mine_0, meas, sem).wait()
    pm = tables[8]
    high, low = split(meas[...])
    high, low = split(dot(pm, high) + dot(pm, low))
    dims = (((1,), (1,)), ((), ()))
    misfit = -(
        lax.dot_general(high, pm, dims, preferred_element_type=F32)
        + lax.dot_general(low, pm, dims, preferred_element_type=F32)
    )
    planes = [x for m in range(2) for x in cmul(load(us, m), load(obj, 1))]
    planes = to_frequency(planes, tables)
    for m, pair in enumerate(modes(planes)):
        re, im = mix(pair, 1.0)
        psi[m, 0] = re
        psi[m, 1] = im
        misfit = misfit + (re * re + im * im)
    meas[...] = misfit
    planes = [
        x for m in range(2) for x in mix((psi[m, 0] * meas[...], psi[m, 1] * meas[...]), -1.0)
    ]
    planes = to_pixels(planes, tables)
    back = []
    total = None
    for m, pair in enumerate(modes(planes)):
        term = cmulc(pair, load(us, m))
        total = term if total is None else (total[0] + term[0], total[1] + term[1])
        back += cmulc(pair, load(obj, 1))
    grad[0, 1] = total[0]
    grad[1, 1] = total[1]
    planes = to_pixels(chirped(cmulc, to_frequency(back, tables)), tables)
    total = None
    for m, pair in enumerate(modes(planes)):
        last = cmulc(pair, load(obj, 0))

        @pl.when(c == m)
        def _():
            mine[0] = last[0]
            mine[1] = last[1]

        @pl.when(c != m)
        def _():
            sib[0] = last[0]
            sib[1] = last[1]

        term = cmulc(pair, (probe[0, m], probe[1, m]))
        total = term if total is None else (total[0] + term[0], total[1] + term[1])
    grad[0, 0] = total[0]
    grad[1, 0] = total[1]


def rows_kernel(plan, g0, g1, before, msg, kept, token, tall):
    y, c = plan[8, 0], plan[8, 1]
    a, b, e = partners(y, c)
    tall[:, :72] = jnp.zeros((4, 72, 256), F32)
    tall[:, 328:] = jnp.zeros((4, 72, 256), F32)
    for w, g in enumerate((g0, g1)):
        core = c if w == 0 else 1 - c
        r = plan[2 * y + core, 2]
        for plane in range(4):
            tall[plane, 72:328] = g[plane // 2, plane % 2]

        def put(out, chip):
            start = jnp.clip(72 + 128 * chip + 64 * c - r, 0, 328)
            row = lax.div(start, 8) * 8
            shift = start - row
            row = pl.multiple_of(row, 8)
            for plane in range(4):
                x = pltpu.roll(tall[plane, pl.ds(row, 72), :], lax.rem(72 - shift, 72), 0)
                out[plane] = x[:64]

        put(msg.at[w, 0], a)
        put(msg.at[w, 1], e)
        put(kept.at[w, 0], y)
        put(kept.at[w, 1], b)
    token[...] = before[...]


def place_kernel(
    plan, kept, got, before, send_edge, send_strip, keep_edge, keep_strip, token, acc
):
    y, c = plan[8, 0], plan[8, 1]
    a, _, _ = partners(y, c)
    acc[...] = jnp.zeros_like(acc)
    for k in range(4):
        ref, w = (kept, k) if k < 2 else (got, k - 2)
        chip = y if k < 2 else a
        core = c if w == 0 else 1 - c
        _, col, _, dc = corner_of(jnp.int32(0), plan[2 * chip + core, 3], 512)
        for d in range(2):
            for plane in range(4):
                x = jnp.concatenate([ref[w, d, plane], jnp.zeros((64, 128), F32)], 1)
                acc[d, plane, :, pl.ds(col, 384)] += pltpu.roll(x, dc, 1)
    keep_strip[...] = acc[0, :, :, :512]
    keep_edge[...] = acc[0, :, :, 512:]
    send_strip[...] = acc[1, :, :, :512]
    send_edge[...] = acc[1, :, :, 512:]
    token[...] = before[...]


def spread_kernel(scale, x, before, out, token):
    total = x[0]
    for k in range(1, x.shape[0]):
        total = total + x[k]
    total = total * scale
    for k in range(out.shape[0]):
        out[k] = total
    token[...] = before[...]


def stack_kernel(core, x, y, out):
    for part in range(2):
        out[part, core[0]] = x[part]
        out[part, 1 - core[0]] = y[part]


def add_kernel(x, y, before, out, token):
    out[...] = x[...] + y[...]
    token[...] = before[...]


def struct(*shape):
    return jax.ShapeDtypeStruct(shape, F32)


SMEM = pl.BlockSpec(memory_space=pltpu.SMEM)
VMEM = pl.BlockSpec(memory_space=pltpu.VMEM)
HBM = pl.BlockSpec(memory_space=pltpu.HBM)
ANY = pl.BlockSpec(memory_space=pl.ANY)


def run_kernel(body, name, ins, in_specs, outs, out_specs, scratch, flops, size, moved=1):
    return pl.pallas_call(
        body,
        out_shape=outs,
        in_specs=in_specs,
        out_specs=out_specs,
        scratch_shapes=scratch,
        compiler_params=pltpu.CompilerParams(vmem_limit_bytes=size << 20),
        cost_estimate=pl.CostEstimate(flops=flops, bytes_accessed=moved << 18, transcendentals=0),
        name=name,
    )(*ins)


def tied(x, *others):
    return pl.pallas_call(
        tie_kernel,
        out_shape=jax.ShapeDtypeStruct(x.shape, x.dtype),
        in_specs=[VMEM] * (1 + len(others)),
        out_specs=VMEM,
        input_output_aliases={0: 0},
        compiler_params=pltpu.CompilerParams(vmem_limit_bytes=4 << 20),
        name="tied",
    )(x, *others)


def pairs(n, f):
    return [(i, f(i)) for i in range(n)]


def core_swap(x):
    return lax.ppermute(x, "c", [(0, 1), (1, 0)])


def y_swap(x, first):
    def partner(i):
        y, c = i // 2, i % 2
        return 2 * ((y ^ 1) if (c == 0) == first else 3 - y) + c

    return lax.ppermute(x, ("y", "c"), pairs(8, partner))


def tile_shift(x, by):
    n = lax.axis_size("z") * lax.axis_size("x")
    return lax.ppermute(x, ("z", "x"), [(i, i + by) for i in range(n) if 0 <= i + by < n])


TOKEN = jax.ShapeDtypeStruct((8, 128), F32)


def spread(x, copies, scale, token):
    _, rows, cols = x.shape

    def body(*refs):
        spread_kernel(scale, *refs)

    return run_kernel(
        body, "spread", (x, token), [VMEM] * 2,
        [struct(copies, rows, cols), TOKEN], [VMEM] * 2, [], 1 << 20, 4,
    )


def added(x, y, token):
    return run_kernel(
        add_kernel, "added", (x, y, token), [VMEM] * 3,
        [struct(*x.shape), TOKEN], [VMEM] * 2, [], 1 << 20, 4,
    )


def shards(object_field, probe, measured, offsets, counts):
    n = probe.shape[-1]
    tables, transfer = make_tables(n)
    y, c = lax.axis_index("y").astype(jnp.int32), lax.axis_index("c").astype(jnp.int32)
    zero = jnp.zeros((), jnp.int32)

    row = 256 * lax.rem(y, 2) + 128 * c
    parts = []
    for layer in range(2):
        part = lax.dynamic_slice(
            object_field, (zero, jnp.int32(layer), row, zero), (2, 1, 128, n)
        ).reshape(2, 128, n)
        parts.append(part)
    parts, measured, offsets, counts = lax.optimization_barrier(
        (parts, measured, offsets, counts)
    )
    halos = [tile_shift(part, -1) for part in parts]

    own_row = jnp.concatenate([counts.reshape(1), offsets.reshape(4), y[None], c[None]])
    own_row = jnp.pad(own_row, (0, 121))
    info = lax.all_to_all(jnp.broadcast_to(own_row, (8, 8, 128)), ("y", "c"), 0, 0, tiled=True)
    own_row = jnp.broadcast_to(own_row, (8, 128))

    mine_0, mine_1 = measured[0, 0, 0], measured[0, 0, 1]
    got_a = y_swap(mine_1, True)
    got_b = y_swap(jnp.stack([mine_1, got_a]), False)
    plan, planned = run_kernel(
        plan_kernel, "plan", (info, own_row), [SMEM] * 2,
        [jax.ShapeDtypeStruct((9, 4), jnp.int32), struct(8, 128)], [SMEM, VMEM],
        [], 1 << 20, 4,
    )
    for_sib = run_kernel(
        pick_kernel, "pick", (plan, mine_1, got_a, got_b), [SMEM, ANY, ANY, ANY],
        struct(n, n), ANY, [pltpu.SemaphoreType.DMA(())], 1 << 20, 4,
    )
    got_sib = core_swap(for_sib)

    pieces = []
    halos[0] = tied(halos[0], planned)
    for got in halos:
        other = y_swap(got, True)
        pieces += [got, other, core_swap(got), core_swap(other)]

    joined = run_kernel(
        join_kernel, "joined", tuple(pieces), [ANY] * 8, struct(8, 128), VMEM, [], LONG, 4,
    )
    grad, mine, sib = run_kernel(
        compute_kernel, "position",
        (plan, joined, object_field, *pieces, probe, mine_0, mine_1, got_a, got_b, got_sib,
         jnp.asarray(tables), jnp.asarray(transfer)),
        [SMEM] + [VMEM] * 11 + [ANY] * 5 + [VMEM] * 2,
        [struct(2, 2, n, n), struct(2, n, n), struct(2, n, n)], [VMEM] * 3,
        [pltpu.VMEM((2, 2, 512, n), F32), pltpu.VMEM((2, 2, 264, 384), F32)]
        + [pltpu.VMEM((2, 2, n, n), F32)] * 3
        + [pltpu.VMEM((n, n), F32), pltpu.SemaphoreType.DMA(())],
        48 * 3 * 2 * n**3, 24, 64,
    )

    grad_sib = core_swap(grad)
    total, token = added(mine, core_swap(sib), jnp.zeros((8, 128), F32))
    pieces_1 = lax.all_to_all(total.reshape(16, 32, n), ("x", "y"), 0, 0, tiled=True)
    msg, kept, token = run_kernel(
        rows_kernel, "rows", (plan, grad, grad_sib, token), [SMEM, VMEM, VMEM, VMEM],
        [struct(2, 2, 4, 64, n)] * 2 + [TOKEN], [VMEM] * 3, [pltpu.VMEM((4, 400, n), F32)],
        1 << 20, 12,
    )
    got = y_swap(msg, True)
    spread_1, token = spread(pieces_1, 8, 1.0, token)
    pieces_2 = lax.all_to_all(spread_1, "z", 0, 0, tiled=True)
    send_edge, send_strip, keep_edge, keep_strip, token = run_kernel(
        place_kernel, "place", (plan, kept, got, token), [SMEM, VMEM, VMEM, VMEM],
        [struct(4, 64, n), struct(4, 64, 512)] * 2 + [TOKEN], [VMEM] * 5,
        [pltpu.VMEM((2, 4, 64, 768), F32)], 1 << 20, 12,
    )
    got_edge = y_swap(send_edge, False)
    got_strip = y_swap(send_strip, False)
    edge, token = added(keep_edge, got_edge, token)
    edge = tile_shift(edge, 1)
    spread_2, token = spread(pieces_2, 16, 1.0 / 16.0, token)
    total = lax.all_to_all(spread_2, ("x", "y"), 0, 0, tiled=True).reshape(2, n, n)
    strip = keep_strip + got_strip
    rows = jnp.concatenate([strip[:, :, :n] + edge, strip[:, :, n:]], 2)
    other = core_swap(total)
    probe_gradient = run_kernel(
        stack_kernel, "stacked", (c[None], total, other), [SMEM, VMEM, VMEM],
        struct(2, 2, n, n), VMEM, [], LONG, 4,
    )
    return rows.reshape(2, 2, 64, 512), probe_gradient


def solution(mesh):
    sizes = (8, 4, 4, 2)
    split_mesh = jax.sharding.Mesh(mesh.devices.reshape(sizes), ("z", "x", "y", "c"))
    tile, scan = ("z", "x"), ("y", "c")
    in_specs = (
        P(None, None, None, tile),
        P(),
        P(tile, scan, None, None, None),
        P(tile, scan, None, None),
        P(tile, scan),
    )
    out_specs = (P(None, None, scan, tile), P())
    return jax.shard_map(
        shards, mesh=split_mesh, in_specs=in_specs, out_specs=out_specs, check_vma=False
    )
```

```python
import math

import jax
import jax.numpy as jnp
import ml_dtypes
import numpy as np
from jax import lax
from jax.experimental import pallas as pl
from jax.experimental.pallas import tpu as pltpu
from jax.sharding import PartitionSpec as P

BF = jnp.bfloat16
F32 = jnp.float32
LONG = 1 << 35


def split_table(table):
    high = table.astype(ml_dtypes.bfloat16)
    low = (table - high.astype(np.float64)).astype(ml_dtypes.bfloat16)
    return high, low


def make_tables(n):
    h = n // 2
    even = np.concatenate([np.arange(0, h, 2), [h], np.arange(n - 2, h, -2)])
    odd = np.concatenate([np.arange(1, h, 2), np.arange(n - 1, h, -2)])
    order = np.concatenate([even, odd])
    pixel = np.arange(n)
    blocks = []
    for rows in (even, odd):
        phase = 2 * np.pi * ((rows[:, None] * pixel[None, :h]) % n) / n
        blocks.append((np.cos(phase) + np.sin(phase)) / math.sqrt(n))

    def square(block):
        high, low = split_table(block)
        half = np.concatenate([high, low], 1)
        return np.concatenate([half, half], 0)

    squares = []
    for block in blocks:
        squares += [square(block.T).T, square(block.T), square(block).T, square(block)]
    perm = np.zeros((n, n))
    perm[pixel, order] = 1
    squares.append(perm.astype(ml_dtypes.bfloat16))
    f = (order + h) % n - h
    q = (f[:, None] ** 2 + f[None, :] ** 2) % (4 * n)
    chirp = 2 * np.pi * q / (4 * n)
    transfer = np.stack([np.cos(chirp), -np.sin(chirp)]).astype(np.float32)
    return np.stack(squares), transfer


def split(x):
    high = x.astype(BF)
    return high, (x - high.astype(F32)).astype(BF)


def dot(a, b):
    return jnp.dot(a, b, preferred_element_type=F32)


def columns_by(x, table):
    high, low = split(x)
    y = dot(jnp.concatenate([high, low], 1), table)
    h = x.shape[1]
    return y[:, :h] + y[:, h:]


def rows_by(table, x):
    high, low = split(x)
    y = dot(table, jnp.concatenate([high, low], 0))
    h = x.shape[0]
    return y[:h] + y[h:]


def to_frequency(planes, tables):
    h = planes[0].shape[0] // 2
    even = [columns_by(x[:, :h] + x[:, h:], tables[1]) for x in planes]
    odd = [columns_by(x[:, :h] - x[:, h:], tables[5]) for x in planes]
    planes = [jnp.concatenate(p, 1) for p in zip(even, odd)]
    even = [rows_by(tables[0], x[:h] + x[h:]) for x in planes]
    odd = [rows_by(tables[4], x[:h] - x[h:]) for x in planes]
    return [jnp.concatenate(p, 0) for p in zip(even, odd)]


def to_pixels(planes, tables):
    h = planes[0].shape[0] // 2
    a = [columns_by(x[:, :h], tables[3]) for x in planes]
    b = [columns_by(x[:, h:], tables[7]) for x in planes]
    planes = [jnp.concatenate([p + q, p - q], 1) for p, q in zip(a, b)]
    a = [rows_by(tables[2], x[:h]) for x in planes]
    b = [rows_by(tables[6], x[h:]) for x in planes]
    return [jnp.concatenate([p + q, p - q], 0) for p, q in zip(a, b)]


def cmul(a, b):
    return a[0] * b[0] - a[1] * b[1], a[0] * b[1] + a[1] * b[0]


def cmulc(a, b):
    return a[0] * b[0] + a[1] * b[1], a[1] * b[0] - a[0] * b[1]


def swap_rows(z):
    q = z.shape[0] // 4
    row = lax.broadcasted_iota(jnp.int32, z.shape, 0)
    fixed = jnp.logical_or(row == 0, row == q)
    turned = jnp.concatenate([z[q : 2 * q], z[:q], z[3 * q :], z[2 * q : 3 * q]], 0)
    return jnp.where(fixed, z, turned)


def swap_cols(z):
    q = z.shape[1] // 4
    even, odd = z[:, : 2 * q], z[:, 2 * q :]
    col = lax.broadcasted_iota(jnp.int32, even.shape, 1)
    fixed = jnp.logical_or(col == 0, col == q)
    even = jnp.where(fixed, even, pltpu.roll(even, q, 1))
    return jnp.concatenate([even, pltpu.roll(odd, q, 1)], 1)


def mix(pair, sign):
    a, b = pair
    ca, cb = swap_cols(a), swap_cols(b)
    re = 0.5 * (sign * (b - swap_rows(cb)) + (swap_rows(a) + ca))
    im = 0.5 * (sign * (swap_rows(ca) - a) + (swap_rows(b) + cb))
    return re, im


def corner_of(r, c, rows):
    row = jnp.minimum(lax.div(r, 8), rows // 8 - 33) * 8
    col = lax.div(c, 128) * 128
    return pl.multiple_of(row, 8), pl.multiple_of(col, 128), r - row, c - col


def rows_down(x, by):
    rows, cols = x.shape
    turned = pltpu.roll(x.reshape(rows // 8, 8, cols), by, 1)
    none = jnp.zeros((1, 8, cols), F32)
    above, here = jnp.concatenate([none, turned], 0), jnp.concatenate([turned, none], 0)
    row = lax.broadcasted_iota(jnp.int32, here.shape, 1)
    return jnp.where(row < by, above, here).reshape(rows + 8, cols)


def rows_up(x, by):
    rows, cols = x.shape
    turned = pltpu.roll(x.reshape(rows // 8, 8, cols), lax.rem(8 - by, 8), 1)
    row = lax.broadcasted_iota(jnp.int32, (rows // 8 - 1, 8, cols), 1)
    return jnp.where(row < 8 - by, turned[:-1], turned[1:]).reshape(rows - 8, cols)


def cols_right(x, by):
    rows, cols = x.shape
    blocks = [pltpu.roll(x[:, k : k + 128], by, 1) for k in range(0, cols, 128)]
    none = jnp.zeros((rows, 128), F32)
    col = lax.broadcasted_iota(jnp.int32, (rows, 128), 1)
    pairs_of = zip([none] + blocks, blocks + [none])
    return jnp.concatenate([jnp.where(col < by, a, b) for a, b in pairs_of], 1)


def cols_left(x, by):
    rows, cols = x.shape
    turn = lax.rem(128 - by, 128)
    blocks = [pltpu.roll(x[:, k : k + 128], turn, 1) for k in range(0, cols, 128)]
    col = lax.broadcasted_iota(jnp.int32, (rows, 128), 1)
    pairs_of = zip(blocks[:-1], blocks[1:])
    return jnp.concatenate([jnp.where(col < 128 - by, a, b) for a, b in pairs_of], 1)


def partners(y, c):
    near, far = jnp.bitwise_xor(y, 1), 3 - y
    return jnp.where(c == 0, near, far), jnp.where(c == 0, far, near), 3 - near


def row_kernel(counts, offsets, place, out):
    lane = lax.broadcasted_iota(jnp.int32, out.shape, 2)
    values = [counts[0, 0]]
    values += [offsets[0, 0, slot, k] for slot in range(2) for k in range(2)]
    row = jnp.zeros(out.shape, jnp.int32)
    for k, value in enumerate(values):
        row = jnp.where(lane == k, value, row)
    out[...] = row


def plan_kernel(info, me, plan):
    count = [info[s, 0, 0] for s in range(8)]
    zeros, doubles = jnp.int32(0), jnp.int32(0)
    zero_rank, double_rank = [], []
    for s in range(8):
        zero_rank.append(zeros)
        double_rank.append(doubles)
        zeros = zeros + (count[s] == 0).astype(jnp.int32)
        doubles = doubles + (count[s] == 2).astype(jnp.int32)
    for s in range(8):
        source = jnp.int32(0)
        for e in range(8):
            taken = jnp.logical_and(count[e] == 2, double_rank[e] == zero_rank[s])
            source = jnp.where(taken, e, source)
        away = count[s] == 0
        source = jnp.where(away, source, s)
        slot = away.astype(jnp.int32)
        plan[s, 0] = source
        plan[s, 1] = slot
        plan[s, 2] = info[source, 0, 1 + 2 * slot]
        plan[s, 3] = info[source, 0, 2 + 2 * slot]
    plan[8, 0] = me[0]
    plan[8, 1] = me[1]


def tie_kernel(*refs):
    pass


def join_kernel(*refs):
    refs[-1][...] = jnp.zeros_like(refs[-1])


def compute_kernel(
    plan, joined, strip, h00, h01, h02, h03, h10, h11, h12, h13, probe,
    mine_0, mine_1, got_a, got_b, sib_1, sib_a, sib_b, tables, transfer,
    grad, mine, sib, halo, full, obj, us, psi, meas, sem,
):
    y, c = plan[8, 0], plan[8, 1]
    own = 2 * y + c
    source, slot = plan[own, 0], plan[own, 1]
    row, col, dr, dc = corner_of(plan[own, 2], plan[own, 3], 512)
    first = lax.div(col, 128)

    a, b, e = partners(y, c)
    core = lax.rem(source, 2)
    chip = lax.div(source, 2)
    here = jnp.logical_and(slot == 1, core == c)
    there = jnp.logical_and(slot == 1, core != c)
    choices = [
        (slot == 0, mine_0),
        (jnp.logical_and(here, chip == y), mine_1),
        (jnp.logical_and(here, chip == a), got_a),
        (jnp.logical_and(here, chip == b), got_b.at[0]),
        (jnp.logical_and(here, chip == e), got_b.at[1]),
        (jnp.logical_and(there, chip == y), sib_1),
        (jnp.logical_and(there, chip == b), sib_a),
        (jnp.logical_and(there, chip == a), sib_b.at[0]),
        (jnp.logical_and(there, chip == e), sib_b.at[1]),
    ]
    for chosen, ref in choices:

        @pl.when(chosen)
        def _():
            pltpu.make_async_copy(ref, meas, sem).start()

    half = lax.rem(y, 2)
    for layer, pieces in enumerate(((h00, h01, h02, h03), (h10, h11, h12, h13))):
        for k, piece in enumerate(pieces):
            hh = half if k % 2 == 0 else 1 - half
            cc = c if k < 2 else 1 - c
            at = pl.multiple_of(256 * hh + 128 * cc, 128)
            halo[:, layer, pl.ds(at, 128), :] = piece[...]
    for i in range(3):

        @pl.when(first + i >= 4)
        def _():
            cols = pl.multiple_of(128 * (first + i - 4), 128)
            full[:, :, :, 128 * i : 128 * (i + 1)] = halo[:, :, pl.ds(row, 264), pl.ds(cols, 128)]

        @pl.when(first + i < 4)
        def _():
            cols = pl.multiple_of(col + 128 * i, 128)
            full[:, :, :, 128 * i : 128 * (i + 1)] = strip[:, :, pl.ds(row, 264), pl.ds(cols, 128)]

    def window(layer):
        for part in range(2):
            obj[layer, part] = rows_up(cols_left(full[part, layer], dc), dr)

    def load(ref, *index):
        return ref[(*index, 0)], ref[(*index, 1)]

    def modes(planes):
        return (planes[0], planes[1]), (planes[2], planes[3])

    def chirped(product, planes):
        h = (transfer[0], transfer[1])
        return [x for pair in modes(planes) for x in product(pair, h)]

    window(0)
    planes = [x for m in range(2) for x in cmul((probe[0, m], probe[1, m]), load(obj, 0))]
    planes = to_pixels(chirped(cmul, to_frequency(planes, tables)), tables)
    for k in range(4):
        us[k // 2, k % 2] = planes[k]
    window(1)
    pltpu.make_async_copy(mine_0, meas, sem).wait()
    pm = tables[8]
    high, low = split(meas[...])
    high, low = split(dot(pm, high) + dot(pm, low))
    dims = (((1,), (1,)), ((), ()))
    misfit = -(
        lax.dot_general(high, pm, dims, preferred_element_type=F32)
        + lax.dot_general(low, pm, dims, preferred_element_type=F32)
    )
    planes = [x for m in range(2) for x in cmul(load(us, m), load(obj, 1))]
    planes = to_frequency(planes, tables)
    for m, pair in enumerate(modes(planes)):
        re, im = mix(pair, 1.0)
        psi[m, 0] = re
        psi[m, 1] = im
        misfit = misfit + (re * re + im * im)
    meas[...] = misfit
    planes = [
        x for m in range(2) for x in mix((psi[m, 0] * meas[...], psi[m, 1] * meas[...]), -1.0)
    ]
    planes = to_pixels(planes, tables)
    back = []
    total = None
    for m, pair in enumerate(modes(planes)):
        term = cmulc(pair, load(us, m))
        total = term if total is None else (total[0] + term[0], total[1] + term[1])
        back += cmulc(pair, load(obj, 1))
    grad[0, 1] = total[0]
    grad[1, 1] = total[1]
    planes = to_pixels(chirped(cmulc, to_frequency(back, tables)), tables)
    total = None
    for m, pair in enumerate(modes(planes)):
        last = cmulc(pair, load(obj, 0))

        @pl.when(c == m)
        def _():
            mine[0] = last[0]
            mine[1] = last[1]

        @pl.when(c != m)
        def _():
            sib[0] = last[0]
            sib[1] = last[1]

        term = cmulc(pair, (probe[0, m], probe[1, m]))
        total = term if total is None else (total[0] + term[0], total[1] + term[1])
    grad[0, 0] = total[0]
    grad[1, 0] = total[1]


def rows_kernel(plan, g0, g1, before, msg, kept, token, tall):
    y, c = plan[8, 0], plan[8, 1]
    a, b, e = partners(y, c)
    tall[:, :64] = jnp.zeros((4, 64, 256), F32)
    tall[:, 328:] = jnp.zeros((4, 64, 256), F32)
    for w, g in enumerate((g0, g1)):
        core = c if w == 0 else 1 - c
        r = plan[2 * y + core, 2]
        dr = lax.rem(r, 8)
        for plane in range(4):
            tall[plane, 64:328] = rows_down(g[plane // 2, plane % 2], dr)

        def put(out, chip):
            start = jnp.clip(64 + 128 * chip + 64 * c - (r - dr), 0, 328)
            out[...] = tall[:, pl.ds(pl.multiple_of(start, 8), 64), :]

        put(msg.at[w, 0], a)
        put(msg.at[w, 1], e)
        put(kept.at[w, 0], y)
        put(kept.at[w, 1], b)
    token[...] = before[...]


def place_kernel(
    plan, kept, got, before, send_edge, send_strip, keep_edge, keep_strip, token, acc
):
    y, c = plan[8, 0], plan[8, 1]
    a, _, _ = partners(y, c)
    acc[...] = jnp.zeros_like(acc)
    for k in range(4):
        ref, w = (kept, k) if k < 2 else (got, k - 2)
        chip = y if k < 2 else a
        core = c if w == 0 else 1 - c
        _, col, _, dc = corner_of(jnp.int32(0), plan[2 * chip + core, 3], 512)
        for d in range(2):
            for plane in range(4):
                acc[d, plane, :, pl.ds(col, 384)] += cols_right(ref[w, d, plane], dc)
    keep_strip[...] = acc[0, :, :, :512]
    keep_edge[...] = acc[0, :, :, 512:]
    send_strip[...] = acc[1, :, :, :512]
    send_edge[...] = acc[1, :, :, 512:]
    token[...] = before[...]


def spread_kernel(scale, x, before, out, token):
    total = x[0]
    for k in range(1, x.shape[0]):
        total = total + x[k]
    total = total * scale
    for k in range(out.shape[0]):
        out[k] = total
    token[...] = before[...]


def stack_kernel(core, x, y, out):
    for part in range(2):
        out[part, core[0]] = x[part]
        out[part, 1 - core[0]] = y[part]


def add_kernel(x, y, before, out, token):
    out[...] = x[...] + y[...]
    token[...] = before[...]


def struct(*shape):
    return jax.ShapeDtypeStruct(shape, F32)


SMEM = pl.BlockSpec(memory_space=pltpu.SMEM)
VMEM = pl.BlockSpec(memory_space=pltpu.VMEM)
HBM = pl.BlockSpec(memory_space=pltpu.HBM)
ANY = pl.BlockSpec(memory_space=pl.ANY)


def run_kernel(body, name, ins, in_specs, outs, out_specs, scratch, flops, size, moved=1):
    return pl.pallas_call(
        body,
        out_shape=outs,
        in_specs=in_specs,
        out_specs=out_specs,
        scratch_shapes=scratch,
        compiler_params=pltpu.CompilerParams(vmem_limit_bytes=size << 20),
        cost_estimate=pl.CostEstimate(flops=flops, bytes_accessed=moved << 18, transcendentals=0),
        name=name,
    )(*ins)


def tied(x, *others):
    return pl.pallas_call(
        tie_kernel,
        out_shape=jax.ShapeDtypeStruct(x.shape, x.dtype),
        in_specs=[VMEM] * (1 + len(others)),
        out_specs=VMEM,
        input_output_aliases={0: 0},
        compiler_params=pltpu.CompilerParams(vmem_limit_bytes=16 << 20),
        name="tied",
    )(x, *others)


def pairs(n, f):
    return [(i, f(i)) for i in range(n)]


def core_swap(x):
    return lax.ppermute(x, "c", [(0, 1), (1, 0)])


def y_swap(x, first):
    def partner(i):
        y, c = i // 2, i % 2
        return 2 * ((y ^ 1) if (c == 0) == first else 3 - y) + c

    return lax.ppermute(x, ("y", "c"), pairs(8, partner))


def tile_shift(x, by):
    n = lax.axis_size("z") * lax.axis_size("x")
    return lax.ppermute(x, ("z", "x"), [(i, i + by) for i in range(n) if 0 <= i + by < n])


TOKEN = jax.ShapeDtypeStruct((8, 128), F32)


def spread(x, copies, scale, token):
    _, rows, cols = x.shape

    def body(*refs):
        spread_kernel(scale, *refs)

    return run_kernel(
        body, "spread", (x, token), [VMEM] * 2,
        [struct(copies, rows, cols), TOKEN], [VMEM] * 2, [], 1 << 20, 4,
    )


def added(x, y, token):
    return run_kernel(
        add_kernel, "added", (x, y, token), [VMEM] * 3,
        [struct(*x.shape), TOKEN], [VMEM] * 2, [], 1 << 20, 4,
    )


def shards(object_field, probe, measured, offsets, counts):
    n = probe.shape[-1]
    tables, transfer = make_tables(n)
    y, c = lax.axis_index("y").astype(jnp.int32), lax.axis_index("c").astype(jnp.int32)
    zero = jnp.zeros((), jnp.int32)

    row = 256 * lax.rem(y, 2) + 128 * c
    parts = []
    for layer in range(2):
        part = lax.dynamic_slice(
            object_field, (zero, jnp.int32(layer), row, zero), (2, 1, 128, n)
        ).reshape(2, 128, n)
        parts.append(part)
    parts, measured, offsets, counts = lax.optimization_barrier(
        (parts, measured, offsets, counts)
    )
    halos = [tile_shift(part, -1) for part in parts]

    place = jnp.stack([y, c])
    own_row = run_kernel(
        row_kernel, "row", (counts, offsets, place), [SMEM] * 3,
        jax.ShapeDtypeStruct((8, 1, 128), jnp.int32), VMEM, [], 1 << 10, 4,
    )
    info = lax.all_to_all(own_row, ("y", "c"), 0, 0, tiled=True)

    mine_0, mine_1 = measured[0, 0, 0], measured[0, 0, 1]
    tables, transfer = jnp.asarray(tables), jnp.asarray(transfer)
    got_a = tied(y_swap(mine_1, True), own_row)
    got_b = y_swap(jnp.stack([mine_1, got_a]), False)
    plan = run_kernel(
        plan_kernel, "plan", (info, place), [SMEM] * 2,
        jax.ShapeDtypeStruct((9, 4), jnp.int32), SMEM, [], 1 << 33, 4,
    )
    sib_maps = [core_swap(x) for x in (mine_1, got_a, got_b)]

    pieces = []
    for got in halos:
        other = y_swap(got, True)
        pieces += [got, other, core_swap(got), core_swap(other)]

    joined = run_kernel(
        join_kernel, "joined", (*pieces, *sib_maps), [ANY] * 11, struct(8, 128), VMEM, [], LONG, 4,
    )
    grad, mine, sib = run_kernel(
        compute_kernel, "position",
        (plan, joined, object_field, *pieces, probe, mine_0, mine_1, got_a, got_b, *sib_maps,
         tables, transfer),
        [SMEM] + [VMEM] * 11 + [ANY] * 7 + [VMEM] * 2,
        [struct(2, 2, n, n), struct(2, n, n), struct(2, n, n)], [VMEM] * 3,
        [pltpu.VMEM((2, 2, 512, n), F32), pltpu.VMEM((2, 2, 264, 384), F32)]
        + [pltpu.VMEM((2, 2, n, n), F32)] * 3
        + [pltpu.VMEM((n, n), F32), pltpu.SemaphoreType.DMA(())],
        48 * 3 * 2 * n**3, 24, 64,
    )

    grad_sib = core_swap(grad)
    total, token = added(mine, core_swap(sib), jnp.zeros((8, 128), F32))
    pieces_1 = lax.all_to_all(total.reshape(16, 32, n), ("x", "y"), 0, 0, tiled=True)
    msg, kept, token = run_kernel(
        rows_kernel, "rows", (plan, grad, grad_sib, token), [SMEM, VMEM, VMEM, VMEM],
        [struct(2, 2, 4, 64, n)] * 2 + [TOKEN], [VMEM] * 3, [pltpu.VMEM((4, 392, n), F32)],
        1 << 20, 12,
    )
    got = y_swap(msg, True)
    spread_1, token = spread(pieces_1, 8, 1.0, token)
    pieces_2 = lax.all_to_all(spread_1, "z", 0, 0, tiled=True)
    send_edge, send_strip, keep_edge, keep_strip, token = run_kernel(
        place_kernel, "place", (plan, kept, got, token), [SMEM, VMEM, VMEM, VMEM],
        [struct(4, 64, n), struct(4, 64, 512)] * 2 + [TOKEN], [VMEM] * 5,
        [pltpu.VMEM((2, 4, 64, 768), F32)], 1 << 20, 12,
    )
    got_edge = y_swap(send_edge, False)
    got_strip = y_swap(send_strip, False)
    edge, token = added(keep_edge, got_edge, token)
    edge = tile_shift(edge, 1)
    spread_2, token = spread(pieces_2, 16, 1.0 / 16.0, token)
    total = lax.all_to_all(spread_2, ("x", "y"), 0, 0, tiled=True).reshape(2, n, n)
    strip = keep_strip + got_strip
    rows = jnp.concatenate([strip[:, :, :n] + edge, strip[:, :, n:]], 2)
    other = core_swap(total)
    probe_gradient = run_kernel(
        stack_kernel, "stacked", (c[None], total, other), [SMEM, VMEM, VMEM],
        struct(2, 2, n, n), VMEM, [], LONG, 4,
    )
    return rows.reshape(2, 2, 64, 512), probe_gradient


def solution(mesh):
    sizes = (8, 4, 4, 2)
    split_mesh = jax.sharding.Mesh(mesh.devices.reshape(sizes), ("z", "x", "y", "c"))
    tile, scan = ("z", "x"), ("y", "c")
    in_specs = (
        P(None, None, None, tile),
        P(),
        P(tile, scan, None, None, None),
        P(tile, scan, None, None),
        P(tile, scan),
    )
    out_specs = (P(None, None, scan, tile), P())
    return jax.shard_map(
        shards, mesh=split_mesh, in_specs=in_specs, out_specs=out_specs, check_vma=False
    )
```

```python
import math

import jax
import jax.numpy as jnp
import ml_dtypes
import numpy as np
from jax import lax
from jax.experimental import pallas as pl
from jax.experimental.pallas import tpu as pltpu
from jax.sharding import PartitionSpec as P

BF = jnp.bfloat16
F32 = jnp.float32
LONG = 1 << 35


def split_table(table):
    high = table.astype(ml_dtypes.bfloat16)
    low = (table - high.astype(np.float64)).astype(ml_dtypes.bfloat16)
    return high, low


def make_tables(n):
    h = n // 2
    even = np.concatenate([np.arange(0, h, 2), [h], np.arange(n - 2, h, -2)])
    odd = np.concatenate([np.arange(1, h, 2), np.arange(n - 1, h, -2)])
    order = np.concatenate([even, odd])
    pixel = np.arange(n)
    blocks = []
    for rows in (even, odd):
        phase = 2 * np.pi * ((rows[:, None] * pixel[None, :h]) % n) / n
        blocks.append((np.cos(phase) + np.sin(phase)) / math.sqrt(n))

    def square(block):
        high, low = split_table(block)
        half = np.concatenate([high, low], 1)
        return np.concatenate([half, half], 0)

    squares = []
    for block in blocks:
        squares += [square(block.T).T, square(block.T), square(block).T, square(block)]
    perm = np.zeros((n, n))
    perm[pixel, order] = 1
    squares.append(perm.astype(ml_dtypes.bfloat16))
    f = (order + h) % n - h
    q = (f[:, None] ** 2 + f[None, :] ** 2) % (4 * n)
    chirp = 2 * np.pi * q / (4 * n)
    transfer = np.stack([np.cos(chirp), -np.sin(chirp)]).astype(np.float32)
    return np.stack(squares), transfer


def split(x):
    high = x.astype(BF)
    return high, (x - high.astype(F32)).astype(BF)


def dot(a, b):
    return jnp.dot(a, b, preferred_element_type=F32)


def columns_by(x, table):
    high, low = split(x)
    y = dot(jnp.concatenate([high, low], 1), table)
    h = x.shape[1]
    return y[:, :h] + y[:, h:]


def rows_by(table, x):
    high, low = split(x)
    y = dot(table, jnp.concatenate([high, low], 0))
    h = x.shape[0]
    return y[:h] + y[h:]


def to_frequency(planes, tables):
    h = planes[0].shape[0] // 2
    even = [columns_by(x[:, :h] + x[:, h:], tables[1]) for x in planes]
    odd = [columns_by(x[:, :h] - x[:, h:], tables[5]) for x in planes]
    planes = [jnp.concatenate(p, 1) for p in zip(even, odd)]
    even = [rows_by(tables[0], x[:h] + x[h:]) for x in planes]
    odd = [rows_by(tables[4], x[:h] - x[h:]) for x in planes]
    return [jnp.concatenate(p, 0) for p in zip(even, odd)]


def to_pixels(planes, tables):
    h = planes[0].shape[0] // 2
    a = [columns_by(x[:, :h], tables[3]) for x in planes]
    b = [columns_by(x[:, h:], tables[7]) for x in planes]
    planes = [jnp.concatenate([p + q, p - q], 1) for p, q in zip(a, b)]
    a = [rows_by(tables[2], x[:h]) for x in planes]
    b = [rows_by(tables[6], x[h:]) for x in planes]
    return [jnp.concatenate([p + q, p - q], 0) for p, q in zip(a, b)]


def cmul(a, b):
    return a[0] * b[0] - a[1] * b[1], a[0] * b[1] + a[1] * b[0]


def cmulc(a, b):
    return a[0] * b[0] + a[1] * b[1], a[1] * b[0] - a[0] * b[1]


def swap_rows(z):
    q = z.shape[0] // 4
    row = lax.broadcasted_iota(jnp.int32, z.shape, 0)
    fixed = jnp.logical_or(row == 0, row == q)
    turned = jnp.concatenate([z[q : 2 * q], z[:q], z[3 * q :], z[2 * q : 3 * q]], 0)
    return jnp.where(fixed, z, turned)


def swap_cols(z):
    q = z.shape[1] // 4
    even, odd = z[:, : 2 * q], z[:, 2 * q :]
    col = lax.broadcasted_iota(jnp.int32, even.shape, 1)
    fixed = jnp.logical_or(col == 0, col == q)
    even = jnp.where(fixed, even, pltpu.roll(even, q, 1))
    return jnp.concatenate([even, pltpu.roll(odd, q, 1)], 1)


def mix(pair, sign):
    a, b = pair
    ca, cb = swap_cols(a), swap_cols(b)
    re = 0.5 * (sign * (b - swap_rows(cb)) + (swap_rows(a) + ca))
    im = 0.5 * (sign * (swap_rows(ca) - a) + (swap_rows(b) + cb))
    return re, im


def corner_of(r, c, rows):
    row = jnp.minimum(lax.div(r, 8), rows // 8 - 33) * 8
    col = lax.div(c, 128) * 128
    return pl.multiple_of(row, 8), pl.multiple_of(col, 128), r - row, c - col


def rows_down(x, by):
    rows, cols = x.shape
    turned = pltpu.roll(x.reshape(rows // 8, 8, cols), by, 1)
    none = jnp.zeros((1, 8, cols), F32)
    above, here = jnp.concatenate([none, turned], 0), jnp.concatenate([turned, none], 0)
    row = lax.broadcasted_iota(jnp.int32, here.shape, 1)
    return jnp.where(row < by, above, here).reshape(rows + 8, cols)


def rows_up(x, by):
    rows, cols = x.shape
    turned = pltpu.roll(x.reshape(rows // 8, 8, cols), lax.rem(8 - by, 8), 1)
    row = lax.broadcasted_iota(jnp.int32, (rows // 8 - 1, 8, cols), 1)
    return jnp.where(row < 8 - by, turned[:-1], turned[1:]).reshape(rows - 8, cols)


def cols_right(x, by):
    rows, cols = x.shape
    blocks = [pltpu.roll(x[:, k : k + 128], by, 1) for k in range(0, cols, 128)]
    none = jnp.zeros((rows, 128), F32)
    col = lax.broadcasted_iota(jnp.int32, (rows, 128), 1)
    pairs_of = zip([none] + blocks, blocks + [none])
    return jnp.concatenate([jnp.where(col < by, a, b) for a, b in pairs_of], 1)


def cols_left(x, by):
    rows, cols = x.shape
    turn = lax.rem(128 - by, 128)
    blocks = [pltpu.roll(x[:, k : k + 128], turn, 1) for k in range(0, cols, 128)]
    col = lax.broadcasted_iota(jnp.int32, (rows, 128), 1)
    pairs_of = zip(blocks[:-1], blocks[1:])
    return jnp.concatenate([jnp.where(col < 128 - by, a, b) for a, b in pairs_of], 1)


def partners(y, c):
    near, far = jnp.bitwise_xor(y, 1), 3 - y
    return jnp.where(c == 0, near, far), jnp.where(c == 0, far, near), 3 - near


def row_kernel(counts, offsets, place, out):
    lane = lax.broadcasted_iota(jnp.int32, out.shape, 2)
    values = [counts[0, 0]]
    values += [offsets[0, 0, slot, k] for slot in range(2) for k in range(2)]
    row = jnp.zeros(out.shape, jnp.int32)
    for k, value in enumerate(values):
        row = jnp.where(lane == k, value, row)
    out[...] = row


def plan_kernel(info, me, plan):
    count = [info[s, 0, 0] for s in range(8)]
    zeros, doubles = jnp.int32(0), jnp.int32(0)
    zero_rank, double_rank = [], []
    for s in range(8):
        zero_rank.append(zeros)
        double_rank.append(doubles)
        zeros = zeros + (count[s] == 0).astype(jnp.int32)
        doubles = doubles + (count[s] == 2).astype(jnp.int32)
    for s in range(8):
        source = jnp.int32(0)
        for e in range(8):
            taken = jnp.logical_and(count[e] == 2, double_rank[e] == zero_rank[s])
            source = jnp.where(taken, e, source)
        away = count[s] == 0
        source = jnp.where(away, source, s)
        slot = away.astype(jnp.int32)
        plan[s, 0] = source
        plan[s, 1] = slot
        plan[s, 2] = info[source, 0, 1 + 2 * slot]
        plan[s, 3] = info[source, 0, 2 + 2 * slot]
    plan[8, 0] = me[0]
    plan[8, 1] = me[1]


def tie_kernel(*refs):
    pass


def join_kernel(*refs):
    refs[-1][...] = jnp.zeros_like(refs[-1])


def compute_kernel(
    plan, joined, strip, h00, h01, h02, h03, h10, h11, h12, h13, probe,
    mine_0, mine_1, got_a, got_b, sib_1, sib_a, sib_b, tables, transfer,
    grad, mine, sib, halo, full, obj, us, psi, meas, sem,
):
    y, c = plan[8, 0], plan[8, 1]
    own = 2 * y + c
    source, slot = plan[own, 0], plan[own, 1]
    row, col, dr, dc = corner_of(plan[own, 2], plan[own, 3], 512)
    first = lax.div(col, 128)

    a, b, e = partners(y, c)
    core = lax.rem(source, 2)
    chip = lax.div(source, 2)
    here = jnp.logical_and(slot == 1, core == c)
    there = jnp.logical_and(slot == 1, core != c)
    choices = [
        (slot == 0, mine_0),
        (jnp.logical_and(here, chip == y), mine_1),
        (jnp.logical_and(here, chip == a), got_a),
        (jnp.logical_and(here, chip == b), got_b.at[0]),
        (jnp.logical_and(here, chip == e), got_b.at[1]),
        (jnp.logical_and(there, chip == y), sib_1),
        (jnp.logical_and(there, chip == b), sib_a),
        (jnp.logical_and(there, chip == a), sib_b.at[0]),
        (jnp.logical_and(there, chip == e), sib_b.at[1]),
    ]
    for chosen, ref in choices:

        @pl.when(chosen)
        def _():
            pltpu.make_async_copy(ref, meas, sem).start()

    half = lax.rem(y, 2)
    for layer, pieces in enumerate(((h00, h01, h02, h03), (h10, h11, h12, h13))):
        for k, piece in enumerate(pieces):
            hh = half if k % 2 == 0 else 1 - half
            cc = c if k < 2 else 1 - c
            at = pl.multiple_of(256 * hh + 128 * cc, 128)
            halo[:, layer, pl.ds(at, 128), :] = piece[...]
    for i in range(3):

        @pl.when(first + i >= 4)
        def _():
            cols = pl.multiple_of(128 * (first + i - 4), 128)
            full[:, :, :, 128 * i : 128 * (i + 1)] = halo[:, :, pl.ds(row, 264), pl.ds(cols, 128)]

        @pl.when(first + i < 4)
        def _():
            cols = pl.multiple_of(col + 128 * i, 128)
            full[:, :, :, 128 * i : 128 * (i + 1)] = strip[:, :, pl.ds(row, 264), pl.ds(cols, 128)]

    def window(layer):
        for part in range(2):
            obj[layer, part] = rows_up(cols_left(full[part, layer], dc), dr)

    def load(ref, *index):
        return ref[(*index, 0)], ref[(*index, 1)]

    def modes(planes):
        return (planes[0], planes[1]), (planes[2], planes[3])

    def chirped(product, planes):
        h = (transfer[0], transfer[1])
        return [x for pair in modes(planes) for x in product(pair, h)]

    window(0)
    planes = [x for m in range(2) for x in cmul((probe[0, m], probe[1, m]), load(obj, 0))]
    planes = to_pixels(chirped(cmul, to_frequency(planes, tables)), tables)
    for k in range(4):
        us[k // 2, k % 2] = planes[k]
    window(1)
    pltpu.make_async_copy(mine_0, meas, sem).wait()
    pm = tables[8]
    high, low = split(meas[...])
    high, low = split(dot(pm, high) + dot(pm, low))
    dims = (((1,), (1,)), ((), ()))
    misfit = -(
        lax.dot_general(high, pm, dims, preferred_element_type=F32)
        + lax.dot_general(low, pm, dims, preferred_element_type=F32)
    )
    planes = [x for m in range(2) for x in cmul(load(us, m), load(obj, 1))]
    planes = to_frequency(planes, tables)
    for m, pair in enumerate(modes(planes)):
        re, im = mix(pair, 1.0)
        psi[m, 0] = re
        psi[m, 1] = im
        misfit = misfit + (re * re + im * im)
    meas[...] = misfit
    planes = [
        x for m in range(2) for x in mix((psi[m, 0] * meas[...], psi[m, 1] * meas[...]), -1.0)
    ]
    planes = to_pixels(planes, tables)
    back = []
    total = None
    for m, pair in enumerate(modes(planes)):
        term = cmulc(pair, load(us, m))
        total = term if total is None else (total[0] + term[0], total[1] + term[1])
        back += cmulc(pair, load(obj, 1))
    grad[0, 1] = total[0]
    grad[1, 1] = total[1]
    planes = to_pixels(chirped(cmulc, to_frequency(back, tables)), tables)
    total = None
    for m, pair in enumerate(modes(planes)):
        last = cmulc(pair, load(obj, 0))

        @pl.when(c == m)
        def _():
            mine[0] = last[0]
            mine[1] = last[1]

        @pl.when(c != m)
        def _():
            sib[0] = last[0]
            sib[1] = last[1]

        term = cmulc(pair, (probe[0, m], probe[1, m]))
        total = term if total is None else (total[0] + term[0], total[1] + term[1])
    grad[0, 0] = total[0]
    grad[1, 0] = total[1]


def rows_kernel(plan, g0, g1, before, msg, kept, token, tall):
    y, c = plan[8, 0], plan[8, 1]
    a, b, e = partners(y, c)
    tall[:, :64] = jnp.zeros((4, 64, 256), F32)
    tall[:, 328:] = jnp.zeros((4, 64, 256), F32)
    for w, g in enumerate((g0, g1)):
        core = c if w == 0 else 1 - c
        r = plan[2 * y + core, 2]
        dr = lax.rem(r, 8)
        for plane in range(4):
            tall[plane, 64:328] = rows_down(g[plane // 2, plane % 2], dr)

        def put(out, chip):
            start = jnp.clip(64 + 128 * chip + 64 * c - (r - dr), 0, 328)
            out[...] = tall[:, pl.ds(pl.multiple_of(start, 8), 64), :]

        put(msg.at[w, 0], a)
        put(msg.at[w, 1], e)
        put(kept.at[w, 0], y)
        put(kept.at[w, 1], b)
    token[...] = before[...]


def place_kernel(
    plan, kept, got, before, send_edge, send_strip, keep_edge, keep_strip, token, acc
):
    y, c = plan[8, 0], plan[8, 1]
    a, _, _ = partners(y, c)
    acc[...] = jnp.zeros_like(acc)
    for k in range(4):
        ref, w = (kept, k) if k < 2 else (got, k - 2)
        chip = y if k < 2 else a
        core = c if w == 0 else 1 - c
        _, col, _, dc = corner_of(jnp.int32(0), plan[2 * chip + core, 3], 512)
        for d in range(2):
            for plane in range(4):
                acc[d, plane, :, pl.ds(col, 384)] += cols_right(ref[w, d, plane], dc)
    keep_strip[...] = acc[0, :, :, :512]
    keep_edge[...] = acc[0, :, :, 512:]
    send_strip[...] = acc[1, :, :, :512]
    send_edge[...] = acc[1, :, :, 512:]
    token[...] = before[...]


def spread_kernel(scale, x, before, out, token):
    total = x[0]
    for k in range(1, x.shape[0]):
        total = total + x[k]
    total = total * scale
    for k in range(out.shape[0]):
        out[k] = total
    token[...] = before[...]


def last_kernel(core, x, y, keep, got, edge, out, rows):
    rows[:, :, :256] = keep[:, :, :256] + got[:, :, :256] + edge[...]
    rows[:, :, 256:] = keep[:, :, 256:] + got[:, :, 256:]
    for part in range(2):
        out[part, core[0]] = x[part]
        out[part, 1 - core[0]] = y[part]


def add_kernel(x, y, before, out, token):
    out[...] = x[...] + y[...]
    token[...] = before[...]


def struct(*shape):
    return jax.ShapeDtypeStruct(shape, F32)


SMEM = pl.BlockSpec(memory_space=pltpu.SMEM)
VMEM = pl.BlockSpec(memory_space=pltpu.VMEM)
HBM = pl.BlockSpec(memory_space=pltpu.HBM)
ANY = pl.BlockSpec(memory_space=pl.ANY)


def run_kernel(body, name, ins, in_specs, outs, out_specs, scratch, flops, size, moved=1):
    return pl.pallas_call(
        body,
        out_shape=outs,
        in_specs=in_specs,
        out_specs=out_specs,
        scratch_shapes=scratch,
        compiler_params=pltpu.CompilerParams(vmem_limit_bytes=size << 20),
        cost_estimate=pl.CostEstimate(flops=flops, bytes_accessed=moved << 18, transcendentals=0),
        name=name,
    )(*ins)


def tied(x, *others):
    return pl.pallas_call(
        tie_kernel,
        out_shape=jax.ShapeDtypeStruct(x.shape, x.dtype),
        in_specs=[VMEM] * (1 + len(others)),
        out_specs=VMEM,
        input_output_aliases={0: 0},
        compiler_params=pltpu.CompilerParams(vmem_limit_bytes=16 << 20),
        name="tied",
    )(x, *others)


def pairs(n, f):
    return [(i, f(i)) for i in range(n)]


def core_swap(x):
    return lax.ppermute(x, "c", [(0, 1), (1, 0)])


def y_swap(x, first):
    def partner(i):
        y, c = i // 2, i % 2
        return 2 * ((y ^ 1) if (c == 0) == first else 3 - y) + c

    return lax.ppermute(x, ("y", "c"), pairs(8, partner))


def tile_shift(x, by):
    n = lax.axis_size("z") * lax.axis_size("x")
    return lax.ppermute(x, ("z", "x"), [(i, i + by) for i in range(n) if 0 <= i + by < n])


TOKEN = jax.ShapeDtypeStruct((8, 128), F32)


def spread(x, copies, scale, token):
    _, rows, cols = x.shape

    def body(*refs):
        spread_kernel(scale, *refs)

    return run_kernel(
        body, "spread", (x, token), [VMEM] * 2,
        [struct(copies, rows, cols), TOKEN], [VMEM] * 2, [], 1 << 20, 4,
    )


def added(x, y, token):
    return run_kernel(
        add_kernel, "added", (x, y, token), [VMEM] * 3,
        [struct(*x.shape), TOKEN], [VMEM] * 2, [], 1 << 20, 4,
    )


def shards(object_field, probe, measured, offsets, counts):
    n = probe.shape[-1]
    tables, transfer = make_tables(n)
    y, c = lax.axis_index("y").astype(jnp.int32), lax.axis_index("c").astype(jnp.int32)
    zero = jnp.zeros((), jnp.int32)

    row = 256 * lax.rem(y, 2) + 128 * c
    parts = []
    for layer in range(2):
        part = lax.dynamic_slice(
            object_field, (zero, jnp.int32(layer), row, zero), (2, 1, 128, n)
        ).reshape(2, 128, n)
        parts.append(part)
    parts, measured, offsets, counts = lax.optimization_barrier(
        (parts, measured, offsets, counts)
    )
    halos = [tile_shift(part, -1) for part in parts]

    place = jnp.stack([y, c])
    own_row = run_kernel(
        row_kernel, "row", (counts, offsets, place), [SMEM] * 3,
        jax.ShapeDtypeStruct((8, 1, 128), jnp.int32), VMEM, [], 1 << 10, 4,
    )
    info = lax.all_to_all(own_row, ("y", "c"), 0, 0, tiled=True)

    mine_0, mine_1 = measured[0, 0, 0], measured[0, 0, 1]
    tables, transfer = jnp.asarray(tables), jnp.asarray(transfer)
    got_a = tied(y_swap(mine_1, True), own_row)
    got_b = y_swap(jnp.stack([mine_1, got_a]), False)
    plan = run_kernel(
        plan_kernel, "plan", (info, place), [SMEM] * 2,
        jax.ShapeDtypeStruct((9, 4), jnp.int32), SMEM, [], 1 << 33, 4,
    )
    sib_maps = [core_swap(x) for x in (mine_1, got_a, got_b)]

    pieces = []
    for got in halos:
        other = y_swap(got, True)
        pieces += [got, other, core_swap(got), core_swap(other)]

    joined = run_kernel(
        join_kernel, "joined", (*pieces, *sib_maps), [ANY] * 11, struct(8, 128), VMEM, [], LONG, 4,
    )
    grad, mine, sib = run_kernel(
        compute_kernel, "position",
        (plan, joined, object_field, *pieces, probe, mine_0, mine_1, got_a, got_b, *sib_maps,
         tables, transfer),
        [SMEM] + [VMEM] * 11 + [ANY] * 7 + [VMEM] * 2,
        [struct(2, 2, n, n), struct(2, n, n), struct(2, n, n)], [VMEM] * 3,
        [pltpu.VMEM((2, 2, 512, n), F32), pltpu.VMEM((2, 2, 264, 384), F32)]
        + [pltpu.VMEM((2, 2, n, n), F32)] * 3
        + [pltpu.VMEM((n, n), F32), pltpu.SemaphoreType.DMA(())],
        48 * 3 * 2 * n**3, 24, 64,
    )

    grad_sib = core_swap(grad)
    total, token = added(mine, core_swap(sib), jnp.zeros((8, 128), F32))
    pieces_1 = lax.all_to_all(total.reshape(16, 32, n), ("x", "y"), 0, 0, tiled=True)
    msg, kept, token = run_kernel(
        rows_kernel, "rows", (plan, grad, grad_sib, token), [SMEM, VMEM, VMEM, VMEM],
        [struct(2, 2, 4, 64, n)] * 2 + [TOKEN], [VMEM] * 3, [pltpu.VMEM((4, 392, n), F32)],
        1 << 20, 12,
    )
    got = y_swap(msg, True)
    spread_1, token = spread(pieces_1, 8, 1.0, token)
    pieces_2 = lax.all_to_all(spread_1, "z", 0, 0, tiled=True)
    send_edge, send_strip, keep_edge, keep_strip, token = run_kernel(
        place_kernel, "place", (plan, kept, got, token), [SMEM, VMEM, VMEM, VMEM],
        [struct(4, 64, n), struct(4, 64, 512)] * 2 + [TOKEN], [VMEM] * 5,
        [pltpu.VMEM((2, 4, 64, 768), F32)], 1 << 20, 12,
    )
    got_edge = y_swap(send_edge, False)
    got_strip = y_swap(send_strip, False)
    edge, token = added(keep_edge, got_edge, token)
    edge = tile_shift(edge, 1)
    spread_2, token = spread(pieces_2, 16, 1.0 / 16.0, token)
    total = lax.all_to_all(spread_2, ("x", "y"), 0, 0, tiled=True).reshape(2, n, n)
    other = core_swap(total)
    probe_gradient, rows = run_kernel(
        last_kernel, "last", (c[None], total, other, keep_strip, got_strip, edge),
        [SMEM] + [VMEM] * 5, [struct(2, 2, n, n), struct(4, 64, 512)], [VMEM] * 2,
        [], 1 << 20, 4,
    )
    return rows.reshape(2, 2, 64, 512), probe_gradient


def solution(mesh):
    sizes = (8, 4, 4, 2)
    split_mesh = jax.sharding.Mesh(mesh.devices.reshape(sizes), ("z", "x", "y", "c"))
    tile, scan = ("z", "x"), ("y", "c")
    in_specs = (
        P(None, None, None, tile),
        P(),
        P(tile, scan, None, None, None),
        P(tile, scan, None, None),
        P(tile, scan),
    )
    out_specs = (P(None, None, scan, tile), P())
    return jax.shard_map(
        shards, mesh=split_mesh, in_specs=in_specs, out_specs=out_specs, check_vma=False
    )
```
